512 devices in a mesh: seq: 32 (over z_hi, x, core), dp: 16 (over z_lo, y).
Axes of the slice: x: 4, y: 4, z: 16 (z_hi: 4, z_lo: 4; z = z_hi * 4 + z_lo), core: 2. Of those that a mesh axis runs over, the one named last changes fastest.
Arguments:
- queries: bfloat16 [16, 2, 2048, 4096], P('dp', None, 'seq'), may hold values from -28 to 28
- span_keys: bfloat16 [16, 2, 2048, 1024], P('dp', None, 'seq'), may hold values from -30 to 30
- span_value_rows: bfloat16 [16, 2, 2048, 1024], P('dp', None, 'seq'), may hold values from -6 to 6
- cache_keys: bfloat16 [16, 128, 1024], P('dp', None, 'seq'), may hold values from -30 to 30
- cached_value_rows: bfloat16 [16, 128, 1024], P('dp', None, 'seq'), may hold values from -6 to 6
- kept_length: int32 [16], P('dp'), may hold values from 16 to 128, as said below
- stream: bfloat16 [16, 2, 2048, 4096], P('dp', None, 'seq'), may hold values from -20 to 20
- norm_gain: float32 [4096], replicated, may hold values from 0.5 to 1.5
- head_weight: bfloat16 [201, 4096], P(None, 'seq'), may hold values from -1 to 1
- returns: float32 [16, 2, 2048], P('dp', None, 'seq'), may hold values from -9.5 to 9.5
Outputs:
- attended: bfloat16 [16, 2, 2048, 4096], P('dp', None, 'seq')
- expected: float32 [16, 2, 2048], P('dp', None, 'seq')
- head_grad: float32 [201, 4096], P(None, 'seq')
The draws below stay inside these ranges and needn't reach their ends.
Inputs may be any that keep to these rules, and one draw needn't show every extreme that they name: Trajectory t keeps its last kept_length[t] cache rows live; some trajectory keeps all 128.
All inputs are finite; a program needn't handle non-finite values.
Results may differ from the reference program's by a relative error of at most 0.022.
Values may be sent and summed in bfloat16 or wider, within the bound.
A program may use at most 64 MiB of HBM per device.

```python
import math
import jax
import jax.numpy as jnp
from jax import lax

D = 4096
QUERY_HEADS = 32
KEY_VALUE_HEADS = 8
HEAD_SIZE = 128
ATOMS = 201
KEPT_POSITIONS = 128
SPAN_COUNT = 2
SPAN_TOKENS = 2048
TRAJECTORY_COUNT = 16


def scaled_keys(noise_key, scale_key, layout_shape, low_scale, high_scale):
    row_scale = jnp.exp(jax.random.uniform(scale_key, layout_shape[:-1] + (1,), jnp.float32, math.log(low_scale), math.log(high_scale)))
    return jax.random.normal(noise_key, layout_shape, jnp.float32) * row_scale


def draw_queries(key, part):
    key = jax.random.fold_in(key, 1)
    layout_shape = (TRAJECTORY_COUNT, SPAN_COUNT, SPAN_TOKENS, D)
    return jax.random.normal(key, layout_shape, jnp.float32).astype(jnp.bfloat16)


def draw_span_keys(key, part):
    key = jax.random.fold_in(key, 2)
    noise_key, scale_key = jax.random.split(key)
    layout_shape = (TRAJECTORY_COUNT, SPAN_COUNT, SPAN_TOKENS, KEY_VALUE_HEADS * HEAD_SIZE)
    return scaled_keys(noise_key, scale_key, layout_shape, 0.4, 4.0).astype(jnp.bfloat16)


def draw_cache_keys(key, part):
    key = jax.random.fold_in(key, 3)
    noise_key, scale_key = jax.random.split(key)
    layout_shape = (TRAJECTORY_COUNT, KEPT_POSITIONS, KEY_VALUE_HEADS * HEAD_SIZE)
    return scaled_keys(noise_key, scale_key, layout_shape, 0.4, 4.0).astype(jnp.bfloat16)


def draw_kept_length(key, part):
    key = jax.random.fold_in(key, 29)
    length_key, full_key = jax.random.split(key)
    lengths = jax.random.randint(length_key, (TRAJECTORY_COUNT,), KEPT_POSITIONS // 8, KEPT_POSITIONS + 1)
    full_at = jax.random.randint(full_key, (), 0, TRAJECTORY_COUNT)
    return jnp.where(jnp.arange(TRAJECTORY_COUNT) == full_at, KEPT_POSITIONS, lengths).astype(jnp.int32)


def draw_stream(key, part):
    key = jax.random.fold_in(key, 4)
    layout_shape = (TRAJECTORY_COUNT, SPAN_COUNT, SPAN_TOKENS, D)
    return jax.random.normal(key, layout_shape, jnp.float32).astype(jnp.bfloat16)


def draw_head_weight(key, part):
    key = jax.random.fold_in(key, 5)
    spread = 3.0 / math.sqrt(D)
    return (jax.random.normal(key, (ATOMS, D), jnp.float32) * spread).astype(jnp.bfloat16)


def shard_levels(own_key, shape, cuts, low, top_value):
    def one(dim, parts):
        steps = jax.random.uniform(jax.random.fold_in(jax.random.fold_in(own_key, 6), dim), (parts,), jnp.float32, low / len(cuts), top_value / len(cuts))
        return jnp.repeat(jnp.exp(steps), shape[dim] // parts).reshape((-1,) + (1,) * (len(shape) - dim - 1))

    gain = one(*cuts[0])
    for cut in cuts[1:]:
        gain = gain * one(*cut)
    return gain


def normal_values(stream_key, extent, scale, reach, cuts=(), held_as=jnp.bfloat16):
    result = jax.random.normal(stream_key, extent, jnp.float32) * scale
    if len(cuts) > 0:
        result = shard_levels(stream_key, extent, cuts, -0.22, 0.18) * result
    return jnp.clip(result, min=-reach, max=reach).astype(held_as)


def setup_inputs(seed: int = 0) -> dict:
    seeds = jax.random.split(jax.random.key(seed), 11)
    return {
        "queries": draw_queries(jax.random.fold_in(seeds[10], 71), 0),
        "span_keys": draw_span_keys(jax.random.fold_in(seeds[10], 71), 0),
        "span_value_rows": normal_values(seeds[2], (TRAJECTORY_COUNT, SPAN_COUNT, SPAN_TOKENS, KEY_VALUE_HEADS * HEAD_SIZE), 1.0, 6.0, ((0, 16), (2, 32))),
        "cache_keys": draw_cache_keys(jax.random.fold_in(seeds[10], 71), 0),
        "cached_value_rows": normal_values(seeds[4], (TRAJECTORY_COUNT, KEPT_POSITIONS, KEY_VALUE_HEADS * HEAD_SIZE), 1.0, 6.0, ((0, 16), (2, 32))),
        "kept_length": draw_kept_length(jax.random.fold_in(seeds[10], 71), 0),
        "stream": draw_stream(jax.random.fold_in(seeds[10], 71), 0),
        "norm_gain": jnp.clip(1.0 + 0.1 * jax.random.normal(seeds[7], (D,), jnp.float32), 0.5, 1.5),
        "head_weight": draw_head_weight(jax.random.fold_in(seeds[10], 71), 0),
        "returns": jnp.clip(jax.random.uniform(seeds[9], (TRAJECTORY_COUNT, SPAN_COUNT, SPAN_TOKENS), jnp.float32, -9.5, 9.5) * shard_levels(seeds[9], (TRAJECTORY_COUNT, SPAN_COUNT, SPAN_TOKENS), ((0, 16), (2, 32)), -0.4, 0.0), -9.5, 9.5),
    }


neg_big = -1e+30
value_low = -10.0
value_high = 10.0
norm_eps = 1e-05

def support_points():
    return value_low + jnp.arange(ATOMS).astype(jnp.float32) * ((value_high - value_low) / (ATOMS - 1))

def attend_head(query_head, key_head, value_head, cache_key, cache_value, kept_one):
    score_scale = 1.0 / math.sqrt(HEAD_SIZE)
    block_rows = min(512, SPAN_TOKENS)
    cache_mask = jnp.arange(KEPT_POSITIONS) >= KEPT_POSITIONS - kept_one
    span_outs = []
    for span_at in range(SPAN_COUNT):
        block_outs = []
        for first_row in range(0, SPAN_TOKENS, block_rows):
            last_row = first_row + block_rows
            key_list = jnp.concatenate([cache_key] + [key_head[past_at] for past_at in range(span_at)] + [key_head[span_at, :last_row]], axis=0)
            value_list = jnp.concatenate([cache_value] + [value_head[past_at] for past_at in range(span_at)] + [value_head[span_at, :last_row]], axis=0)
            scores = jnp.dot(query_head[span_at, first_row:last_row], key_list.T, preferred_element_type=jnp.float32) * score_scale
            causal = jnp.arange(last_row)[None, :] <= (first_row + jnp.arange(block_rows))[:, None]
            allowed = jnp.concatenate([jnp.broadcast_to(cache_mask[None, :], (block_rows, KEPT_POSITIONS)), jnp.ones((block_rows, span_at * SPAN_TOKENS), dtype=jnp.bool_), causal], axis=1)
            scores = jnp.where(allowed, scores, neg_big)
            row_top = lax.optimization_barrier(jnp.max(scores, axis=1, keepdims=True))
            exponent = jnp.where(allowed, jnp.exp(scores - row_top), 0.0)
            total = lax.optimization_barrier(jnp.sum(exponent, axis=1, keepdims=True))
            weights = exponent.astype(jnp.bfloat16)
            summed = jnp.dot(weights, value_list, preferred_element_type=jnp.float32)
            block_outs.append((summed / total).astype(jnp.bfloat16))
        span_outs.append(jnp.concatenate(block_outs, axis=0))
    return jnp.stack(span_outs)

def reference(queries, span_keys, span_value_rows, cache_keys, cached_value_rows, kept_length, stream, norm_gain, head_weight, returns):
    group_portion = QUERY_HEADS // KEY_VALUE_HEADS
    points = support_points()
    spacing = (value_high - value_low) / (ATOMS - 1)
    row_count = SPAN_COUNT * SPAN_TOKENS

    def one_trajectory(grad_sum, inputs):
        query_one, single_key, single_value, single_cached_key, single_cached_value, kept_one, stream_one, return_one = inputs
        query_heads = jnp.transpose(query_one.reshape(SPAN_COUNT, SPAN_TOKENS, QUERY_HEADS, HEAD_SIZE), (2, 0, 1, 3))
        head_keys = jnp.transpose(single_key.reshape(SPAN_COUNT, SPAN_TOKENS, KEY_VALUE_HEADS, HEAD_SIZE), (2, 0, 1, 3))
        head_values = jnp.transpose(single_value.reshape(SPAN_COUNT, SPAN_TOKENS, KEY_VALUE_HEADS, HEAD_SIZE), (2, 0, 1, 3))
        cached_key_heads = jnp.transpose(single_cached_key.reshape(KEPT_POSITIONS, KEY_VALUE_HEADS, HEAD_SIZE), (1, 0, 2))
        cached_value_heads = jnp.transpose(single_cached_value.reshape(KEPT_POSITIONS, KEY_VALUE_HEADS, HEAD_SIZE), (1, 0, 2))

        def per_head(head_at):
            kv_group = head_at // group_portion
            return attend_head(query_heads[head_at], head_keys[kv_group], head_values[kv_group], cached_key_heads[kv_group], cached_value_heads[kv_group], kept_one)
        head_outs = lax.map(per_head, jnp.arange(QUERY_HEADS).astype(jnp.int32))
        attended_one = jnp.transpose(head_outs, (1, 2, 0, 3)).reshape(SPAN_COUNT, SPAN_TOKENS, D)
        mixed_rows = (stream_one.astype(jnp.float32) + attended_one.astype(jnp.float32)).reshape(row_count, D)
        mean_square = lax.optimization_barrier(jnp.mean(mixed_rows * mixed_rows, axis=1, keepdims=True))
        normed = (mixed_rows * lax.rsqrt(mean_square + norm_eps) * norm_gain).astype(jnp.bfloat16)
        logits = lax.dot_general(head_weight, normed, (((1,), (1,)), ((), ())), preferred_element_type=jnp.float32)
        row_top = lax.optimization_barrier(jnp.max(logits, axis=0, keepdims=True))
        exponent = jnp.exp(logits - row_top)
        atom_probs = exponent / lax.optimization_barrier(jnp.sum(exponent, axis=0, keepdims=True))
        expected_one = lax.optimization_barrier(jnp.sum(atom_probs * points[:, None], axis=0))
        target = jnp.maximum(0.0, 1.0 - jnp.abs(return_one.reshape(row_count)[None, :] - points[:, None]) / spacing)
        atom_error = (atom_probs - target).astype(jnp.bfloat16)
        grad_sum = grad_sum + jnp.dot(atom_error, normed, preferred_element_type=jnp.float32)
        return (grad_sum, (attended_one, expected_one.reshape(SPAN_COUNT, SPAN_TOKENS)))
    grad_sum, (attended, expected) = lax.scan(one_trajectory, jnp.zeros((ATOMS, D), jnp.float32), (queries, span_keys, span_value_rows, cache_keys, cached_value_rows, kept_length, stream, returns))
    head_grad = grad_sum * (1.0 / math.sqrt(TRAJECTORY_COUNT * SPAN_COUNT * SPAN_TOKENS))
    return (attended, expected, head_grad)
```

```python
import functools
import math

import jax
import jax.numpy as jnp
from jax import lax
from jax.experimental import pallas as pl
from jax.experimental.pallas import tpu as pltpu
from jax.sharding import PartitionSpec as P

D = 4096
QUERY_HEADS = 32
KEY_VALUE_HEADS = 8
HEAD_SIZE = 128
ATOMS = 201
ATOM_ROWS = 256
KEPT = 128
SPANS = 2
TOKENS = 64
REGION = 512
GROUP = 4
WIDE = GROUP * HEAD_SIZE

neg_big = -1e30
value_low = -10.0
value_high = 10.0
norm_eps = 1e-05
SPACING = (value_high - value_low) / (ATOMS - 1)
EXP_SCALE = math.log2(math.e) / math.sqrt(HEAD_SIZE)
SUM_LANE = ATOM_ROWS - 1
MESH = pl.DeviceIdType.MESH
F32 = jnp.float32
BF16 = jnp.bfloat16


def dot_nt(a, b):
    return lax.dot_general(a, b, (((1,), (1,)), ((), ())), preferred_element_type=F32)


def dot_nn(a, b):
    return lax.dot_general(a, b, (((1,), (0,)), ((), ())), preferred_element_type=F32)


def dot_tn(a, b):
    return lax.dot_general(a, b, (((0,), (0,)), ((), ())), preferred_element_type=F32)


def aligned(index, step):
    return pl.ds(pl.multiple_of(index * step, step), step)


def loop(low, high, body):
    def step(index, carry):
        body(index)
        return carry

    lax.fori_loop(low, high, step, jnp.int32(0))


def settle(ref, sem):
    pltpu.make_async_copy(ref, ref, sem).wait()


def kernel(
    q_in, k_in, v_in, ck_in, cv_in, kept_ref, st_in, gain_ref, hw_ref, ret_ref,
    att_out, exp_out, hg_out,
    qbuf, kbuf, vbuf, stbuf, ckp, cvp, ckbuf, cvbuf, hwp, hwq,
    top, acc, obuf, mg, lpart, lslot, errown, errbuf, gacc, gsend, yrecv,
    zsend, zrecv, fsend, fin,
    xs, xr, cs, cr, hs, hr, hys, hyr, zs, zr, os, orr, ls, lr, es, er, gs, gr,
):
    seq = lax.axis_index("seq")
    dp = lax.axis_index("dp")
    g = lax.rem(seq, 8)
    zh = lax.div(seq, 8)
    y = lax.rem(dp, 4)
    zl = lax.div(dp, 4)
    zi = zh * 4 + zl
    head = lax.div(seq, 4)
    piece = lax.rem(seq, 4)
    owner = 4 * g + y
    is_owner = owner == seq

    barrier = pltpu.get_barrier_semaphore()

    def greet(to_seq, to_dp):
        pl.semaphore_signal(
            barrier, inc=1, device_id={"seq": to_seq, "dp": to_dp}, device_id_type=MESH
        )

    loop(1, 32, lambda i: greet(lax.rem(seq + i, 32), dp))
    loop(1, 4, lambda i: greet(seq, zl * 4 + lax.rem(y + i, 4)))

    def greet_z(i):
        a = lax.div(i, 3)
        b = lax.rem(i, 3) + 1
        greet(a * 8 + g, lax.rem(zl + b, 4) * 4 + y)

    loop(0, 12, greet_z)

    def greet_source(i):
        from_seq = lax.div(i, 4) * 8 + head
        from_dp = lax.rem(i, 4) * 4 + piece

        @pl.when(jnp.logical_not(jnp.logical_and(from_seq == seq, from_dp == dp)))
        def _():
            greet(from_seq, from_dp)

    loop(0, 16, greet_source)
    pl.semaphore_wait(barrier, 62 - is_owner.astype(jnp.int32))

    def remote(src, dst, send_sem, recv_sem, to_seq, to_dp=None):
        pltpu.make_async_remote_copy(
            src_ref=src, dst_ref=dst, send_sem=send_sem, recv_sem=recv_sem,
            device_id={"seq": to_seq, "dp": dp if to_dp is None else to_dp},
            device_id_type=MESH,
        ).start()

    def local(src, dst, sem):
        pltpu.make_async_copy(src, dst, sem).start()

    def spread(src, dst, width, c, t):
        def one(i):
            to = lax.rem(g + i, 8)
            remote(
                src.at[0, c, :, aligned(to, width)], dst.at[aligned(g, TOKENS), :],
                xs.at[t], xr.at[t], zh * 8 + to,
            )

        loop(1, 8, one)
        local(src.at[0, c, :, aligned(g, width)], dst.at[aligned(g, TOKENS), :], xr.at[t])

    right = lax.rem(zh + 1, 4) * 8 + g
    left = lax.rem(zh + 3, 4) * 8 + g

    def send_own(buf, c, kind):
        remote(buf.at[0, c], buf.at[1, c], zs.at[0, c, kind], zr.at[0, c, kind], right)
        remote(buf.at[0, c], buf.at[2, c], zs.at[1, c, kind], zr.at[1, c, kind], left)

    spread(k_in, kbuf.at[0, 0], HEAD_SIZE, 0, 0)
    spread(v_in, vbuf.at[0, 0], HEAD_SIZE, 0, 1)

    hwp[...] = jnp.zeros_like(hwp)
    hwp[0:ATOMS, :] = hw_ref[...]

    def hand_out(i):
        to = i * 8 + head
        mine = to == seq
        rows = aligned(y, 64)

        @pl.when(jnp.logical_not(mine))
        def _():
            remote(ck_in.at[0], ckp.at[piece], cs.at[0], cr.at[0], to)
            remote(cv_in.at[0], cvp.at[piece], cs.at[1], cr.at[1], to)
            remote(hwp.at[rows, :], hwq.at[y, piece], hs.at[0], hr.at[0], to)

        @pl.when(mine)
        def _():
            local(ck_in.at[0], ckp.at[piece], cr.at[0])
            local(cv_in.at[0], cvp.at[piece], cr.at[1])
            local(hwp.at[rows, :], hwq.at[y, piece], hr.at[0])

    loop(0, 4, hand_out)

    settle(kbuf.at[0, 0], xr.at[0])
    send_own(kbuf, 0, 0)
    settle(vbuf.at[0, 0], xr.at[1])
    send_own(vbuf, 0, 1)
    spread(k_in, kbuf.at[0, 1], HEAD_SIZE, 1, 2)
    spread(v_in, vbuf.at[0, 1], HEAD_SIZE, 1, 3)
    spread(q_in, qbuf.at[0], WIDE, 0, 4)
    spread(q_in, qbuf.at[1], WIDE, 1, 5)
    settle(kbuf.at[0, 1], xr.at[2])
    send_own(kbuf, 1, 0)
    settle(vbuf.at[0, 1], xr.at[3])
    send_own(vbuf, 1, 1)
    spread(st_in, stbuf.at[0], WIDE, 0, 6)
    spread(st_in, stbuf.at[1], WIDE, 1, 7)

    ones = jnp.ones((REGION, HEAD_SIZE), BF16)

    def query(c, h):
        return qbuf[c, :, aligned(h, HEAD_SIZE)]

    def start_rows(c, h, scores, values, summing):
        now = jnp.broadcast_to(jnp.max(scores, axis=1, keepdims=True), (REGION, HEAD_SIZE))
        weights = jnp.exp2(scores - now).astype(BF16)
        acc[c, h] = dot_nn(weights, jnp.concatenate([values, summing], axis=1))
        top[c, h] = now

    def add_rows(c, h, scores, values):
        old = top[c, h]
        now = jnp.maximum(old, jnp.max(scores, axis=1, keepdims=True))
        shrink = jnp.exp2(old - now)
        weights = jnp.exp2(scores - jnp.concatenate([now] * 4, axis=1)).astype(BF16)
        added = dot_nn(weights, jnp.concatenate([values, ones], axis=1))
        acc[c, h] = acc[c, h] * jnp.concatenate([shrink, shrink], axis=1) + added
        top[c, h] = now

    def full_block(c, slot, past):
        def one(h):
            scores = dot_nt(query(c, h), kbuf[slot, past]) * EXP_SCALE
            add_rows(c, h, scores, vbuf[slot, past])

        loop(0, GROUP, one)

    def own_block(i):
        c = lax.div(i, GROUP)
        h = lax.rem(i, GROUP)
        scores = dot_nt(query(c, h), ckbuf[...]) * EXP_SCALE
        position = lax.broadcasted_iota(jnp.int32, scores.shape, 1)
        scores = jnp.where(position >= KEPT - kept_ref[0], scores, neg_big)
        start_rows(c, h, scores, cvbuf[...], ones[:KEPT])
        scores = dot_nt(query(c, h), kbuf[0, c]) * EXP_SCALE
        row = lax.broadcasted_iota(jnp.int32, scores.shape, 0)
        column = lax.broadcasted_iota(jnp.int32, scores.shape, 1)
        scores = jnp.where(column <= row, scores, neg_big)
        add_rows(c, h, scores, vbuf[0, c])

    settle(ckp, cr.at[0])
    settle(cvp, cr.at[1])
    for parts, whole in ((ckp, ckbuf), (cvp, cvbuf)):
        joined = jnp.zeros((KEPT, HEAD_SIZE), F32)
        for j in range(4):
            place = lax.broadcasted_iota(jnp.int32, (32, HEAD_SIZE), 0) + 32 * j
            lane = lax.broadcasted_iota(jnp.int32, (32, HEAD_SIZE), 1)
            joined = joined + dot_nn(parts[j], (place == lane).astype(BF16))
        whole[...] = joined.astype(BF16)

    settle(hwq.at[y], hr.at[0])

    def share_head(i):
        remote(
            hwq.at[y], hwq.at[y], hys.at[0], hyr.at[0], seq, zl * 4 + lax.rem(y + i, 4)
        )

    loop(1, 4, share_head)

    settle(qbuf.at[0], xr.at[4])
    settle(qbuf.at[1], xr.at[5])
    loop(0, SPANS * GROUP, own_block)
    full_block(1, 0, 0)

    def arrive(slot, past):
        settle(kbuf.at[slot, past], zr.at[slot - 1, past, 0])
        settle(vbuf.at[slot, past], zr.at[slot - 1, past, 1])
        if slot == 1:
            remote(
                kbuf.at[1, past], kbuf.at[3, past], zs.at[2, past, 0], zr.at[2, past, 0], right
            )
        if slot == 2:
            remote(
                vbuf.at[2, past], vbuf.at[3, past], zs.at[2, past, 1], zr.at[2, past, 1], left
            )

    def use(slot, past):
        source = lax.rem(zh + (3, 1, 2)[slot - 1], 4)
        earlier = (source < zh).astype(jnp.int32)
        first = 1 - earlier if past == 0 else 1
        last = 2 if past == 0 else 1 + earlier
        loop(first, last, lambda c: full_block(c, slot, past))

    def finish(c):
        settle(stbuf.at[c], xr.at[6 + c])
        squares = jnp.zeros((REGION, 1), F32)
        logits = jnp.zeros((REGION, ATOM_ROWS), F32)
        for h in range(GROUP):
            rows = acc[c, h]
            columns = slice(h * HEAD_SIZE, (h + 1) * HEAD_SIZE)
            out = (rows[:, :HEAD_SIZE] / rows[:, HEAD_SIZE:]).astype(BF16)
            obuf[c, :, columns] = out
            mixed = stbuf[c, :, columns].astype(F32) + out.astype(F32)
            squares = squares + jnp.sum(mixed * mixed, axis=1, keepdims=True)
            gain = gain_ref[:, aligned(g * GROUP + h, HEAD_SIZE)]
            scaled = (mixed * gain).astype(BF16)
            mg[c, :, columns] = scaled
            head_rows = jnp.concatenate([hwq[j, h] for j in range(4)], axis=0)
            logits = logits + dot_nt(scaled, head_rows)
        lane = lax.broadcasted_iota(jnp.int32, logits.shape, 1)
        lpart[c] = jnp.where(lane == SUM_LANE, squares, logits)

        def send_logits(i):
            to = lax.rem(g + i, 8)
            remote(
                lpart.at[c, aligned(to, TOKENS), :], lslot.at[c, g],
                ls.at[c], lr.at[c], zh * 8 + to,
            )

        loop(1, 8, send_logits)
        local(lpart.at[c, aligned(g, TOKENS), :], lslot.at[c, g], lr.at[c])

        def send_out(i):
            to = lax.rem(g + i, 8)
            remote(
                obuf.at[c, aligned(to, TOKENS), :], att_out.at[0, c, :, aligned(g, WIDE)],
                os.at[c], orr.at[c], zh * 8 + to,
            )

        loop(1, 8, send_out)
        local(
            obuf.at[c, aligned(g, TOKENS), :], att_out.at[0, c, :, aligned(g, WIDE)], orr.at[c]
        )

    def value_head(c):
        settle(lslot.at[c], lr.at[c])
        total = lslot[c, 0]
        for i in range(1, 8):
            total = total + lslot[c, i]
        lane = lax.broadcasted_iota(jnp.int32, total.shape, 1)
        squares = jnp.sum(jnp.where(lane == SUM_LANE, total, 0.0), axis=1, keepdims=True)
        scale = lax.rsqrt(squares / D + norm_eps)
        atom = lane < ATOMS
        logits = jnp.where(atom, total * scale, neg_big)
        exponent = jnp.exp(logits - jnp.max(logits, axis=1, keepdims=True))
        probs = exponent / jnp.sum(exponent, axis=1, keepdims=True)
        points = value_low + lane.astype(F32) * SPACING
        expected = jnp.sum(jnp.where(atom, probs * points, 0.0), axis=1, keepdims=True)
        same = lax.broadcasted_iota(jnp.int32, (TOKENS, TOKENS), 0) == lax.broadcasted_iota(
            jnp.int32, (TOKENS, TOKENS), 1
        )
        exp_out[0, c : c + 1, :] = jnp.sum(
            jnp.where(same, expected, 0.0), axis=0, keepdims=True
        )
        returns = jnp.sum(
            jnp.where(same, ret_ref[0, c : c + 1, :], 0.0), axis=1, keepdims=True
        )
        target = jnp.maximum(0.0, 1.0 - jnp.abs(returns - points) / SPACING)
        error = jnp.where(atom, probs - target, 0.0)
        errown[c] = (error * scale).astype(BF16)

        def send_error(i):
            to = lax.rem(g + i, 8)
            remote(
                errown.at[c], errbuf.at[c, aligned(g, TOKENS), :],
                es.at[c], er.at[c], zh * 8 + to,
            )

        loop(1, 8, send_error)
        local(errown.at[c], errbuf.at[c, aligned(g, TOKENS), :], er.at[c])

    for slot in (1, 2):
        arrive(slot, 0)
        use(slot, 0)
    for slot in (1, 2):
        arrive(slot, 1)
        use(slot, 1)
    arrive(3, 0)
    use(3, 0)
    settle(hwq.at[pl.ds(0, 3)], hyr.at[0])
    finish(0)
    value_head(0)
    arrive(3, 1)
    use(3, 1)
    finish(1)
    settle(errbuf.at[0], er.at[0])
    gacc[...] = dot_tn(errbuf[0], mg[0])
    value_head(1)
    settle(errbuf.at[1], er.at[1])

    for j in range(4):
        columns = slice(j * HEAD_SIZE, (j + 1) * HEAD_SIZE)
        gsend[j] = (gacc[:, columns] + dot_tn(errbuf[1], mg[1, :, columns])).astype(BF16)

    def send_y(i):
        to = lax.rem(y + i, 4)
        remote(gsend.at[to], yrecv.at[y], gs.at[0], gr.at[0], seq, zl * 4 + to)

    loop(1, 4, send_y)
    local(gsend.at[y], yrecv.at[y], gr.at[0])
    settle(yrecv, gr.at[0])
    zsend[...] = (
        (yrecv[0].astype(F32) + yrecv[1].astype(F32))
        + (yrecv[2].astype(F32) + yrecv[3].astype(F32))
    ).astype(BF16)

    def send_z(i):
        to = lax.rem(zi + i, 16)
        remote(
            zsend.at[aligned(to, 16), :], zrecv.at[zi], gs.at[1], gr.at[1],
            lax.div(to, 4) * 8 + g, lax.rem(to, 4) * 4 + y,
        )

    loop(1, 16, send_z)
    local(zsend.at[aligned(zi, 16), :], zrecv.at[zi], gr.at[1])
    settle(zrecv, gr.at[1])
    summed = zrecv[0].astype(F32)
    for i in range(1, 16):
        summed = summed + zrecv[i].astype(F32)
    fsend[...] = summed * (1.0 / math.sqrt(16 * SPANS * 2048))

    def send_final(i):
        mine = jnp.logical_and(is_owner, i == dp)

        @pl.when(jnp.logical_not(mine))
        def _():
            remote(fsend, fin.at[aligned(zi, 16), :], gs.at[2], gr.at[2], owner, i)

        @pl.when(mine)
        def _():
            local(fsend, fin.at[aligned(zi, 16), :], gr.at[2])

    loop(0, 16, send_final)
    settle(fin, gr.at[2])
    hg_out[...] = fin[0:ATOMS, :]

    for c in range(SPANS):
        settle(att_out.at[0, c], orr.at[c])
        settle(obuf.at[c, pl.ds(0, 448), :], os.at[c])
        settle(lslot.at[c, pl.ds(0, 7)], ls.at[c])
        settle(errbuf.at[c, pl.ds(0, 448), :], es.at[c])
        for kind, buf in ((0, kbuf), (1, vbuf)):
            settle(buf.at[0, c, pl.ds(0, 448), :], xs.at[2 * c + kind])
            for way in range(3):
                settle(buf.at[0, c], zs.at[way, c, kind])
        settle(qbuf.at[c, pl.ds(0, 448), :], xs.at[4 + c])
        settle(stbuf.at[c, pl.ds(0, 448), :], xs.at[6 + c])
    sent_head = lax.div(seq, 4) == lax.rem(seq, 8)

    def settle_pieces(count):
        settle(ckp.at[pl.ds(0, count)], cs.at[0])
        settle(cvp.at[pl.ds(0, count)], cs.at[1])
        settle(hwq.at[0, pl.ds(0, count)], hs.at[0])

    pl.when(sent_head)(lambda: settle_pieces(3))
    pl.when(jnp.logical_not(sent_head))(lambda: settle_pieces(4))
    settle(hwq.at[pl.ds(0, 3)], hys.at[0])
    settle(yrecv.at[pl.ds(0, 3)], gs.at[0])
    settle(zrecv.at[pl.ds(0, 15)], gs.at[1])
    pl.when(is_owner)(lambda: settle(fin.at[pl.ds(0, 240), :], gs.at[2]))
    pl.when(jnp.logical_not(is_owner))(lambda: settle(fin, gs.at[2]))


def on_device(
    queries, span_keys, span_value_rows, cache_keys, cached_value_rows,
    kept_length, stream, norm_gain, head_weight, returns,
):
    anywhere = pl.BlockSpec(memory_space=pl.ANY)
    vmem = pl.BlockSpec(memory_space=pltpu.VMEM)
    smem = pl.BlockSpec(memory_space=pltpu.SMEM)
    dma = pltpu.SemaphoreType.DMA
    return pl.pallas_call(
        kernel,
        out_shape=(
            jax.ShapeDtypeStruct((1, SPANS, TOKENS, D), BF16),
            jax.ShapeDtypeStruct((1, SPANS, TOKENS), F32),
            jax.ShapeDtypeStruct((ATOMS, HEAD_SIZE), F32),
        ),
        in_specs=[
            anywhere, anywhere, anywhere, anywhere, anywhere, smem, anywhere, vmem, vmem, vmem,
        ],
        out_specs=(anywhere, vmem, vmem),
        scratch_shapes=[
            pltpu.VMEM((SPANS, REGION, WIDE), BF16),
            pltpu.VMEM((4, SPANS, REGION, HEAD_SIZE), BF16),
            pltpu.VMEM((4, SPANS, REGION, HEAD_SIZE), BF16),
            pltpu.VMEM((SPANS, REGION, WIDE), BF16),
            pltpu.VMEM((4, KEPT, 32), BF16),
            pltpu.VMEM((4, KEPT, 32), BF16),
            pltpu.VMEM((KEPT, HEAD_SIZE), BF16),
            pltpu.VMEM((KEPT, HEAD_SIZE), BF16),
            pltpu.VMEM((ATOM_ROWS, HEAD_SIZE), BF16),
            pltpu.VMEM((4, 4, 64, HEAD_SIZE), BF16),
            pltpu.VMEM((SPANS, GROUP, REGION, HEAD_SIZE), F32),
            pltpu.VMEM((SPANS, GROUP, REGION, 2 * HEAD_SIZE), F32),
            pltpu.VMEM((SPANS, REGION, WIDE), BF16),
            pltpu.VMEM((SPANS, REGION, WIDE), BF16),
            pltpu.VMEM((SPANS, REGION, ATOM_ROWS), F32),
            pltpu.VMEM((SPANS, 8, TOKENS, ATOM_ROWS), F32),
            pltpu.VMEM((SPANS, TOKENS, ATOM_ROWS), BF16),
            pltpu.VMEM((SPANS, REGION, ATOM_ROWS), BF16),
            pltpu.VMEM((ATOM_ROWS, WIDE), F32),
            pltpu.VMEM((4, ATOM_ROWS, HEAD_SIZE), BF16),
            pltpu.VMEM((4, ATOM_ROWS, HEAD_SIZE), BF16),
            pltpu.VMEM((ATOM_ROWS, HEAD_SIZE), BF16),
            pltpu.VMEM((16, 16, HEAD_SIZE), BF16),
            pltpu.VMEM((16, HEAD_SIZE), F32),
            pltpu.VMEM((ATOM_ROWS, HEAD_SIZE), F32),
            dma((8,)), dma((8,)),
            dma((2,)), dma((2,)),
            dma((1,)), dma((1,)),
            dma((1,)), dma((1,)),
            dma((3, 2, 2)), dma((3, 2, 2)),
            dma((2,)), dma((2,)),
            dma((2,)), dma((2,)),
            dma((2,)), dma((2,)),
            dma((3,)), dma((3,)),
        ],
        compiler_params=pltpu.CompilerParams(
            collective_id=0, has_side_effects=True, vmem_limit_bytes=48 * 1024 * 1024
        ),
    )(
        queries, span_keys, span_value_rows, cache_keys, cached_value_rows,
        kept_length, stream, norm_gain.reshape(1, D), head_weight, returns,
    )


def solution(mesh):
    return jax.shard_map(
        on_device,
        mesh=mesh,
        in_specs=(
            P("dp", None, "seq", None),
            P("dp", None, "seq", None),
            P("dp", None, "seq", None),
            P("dp", None, "seq"),
            P("dp", None, "seq"),
            P("dp"),
            P("dp", None, "seq", None),
            P(),
            P(None, "seq"),
            P("dp", None, "seq"),
        ),
        out_specs=(P("dp", None, "seq", None), P("dp", None, "seq"), P(None, "seq")),
        check_vma=False,
    )
```
